128 devices in a mesh: leaf: 8 (over x, core), front: 16 (over y, z).
Axes of the slice: x: 4, y: 4, z: 4, core: 2. Of those that a mesh axis runs over, the one named last changes fastest.
Arguments:
- tiles: bfloat16 [2, 8, 16, 24, 128, 128], P(None, 'leaf', 'front'), may hold values from -2304 to 2304, as said below
- tile_pos: int32 [2, 8, 16, 2, 24], P(None, 'leaf'), may hold values from 0 to 31, as said below
- diag: float32 [2, 8, 4096], P(None, 'leaf', 'front'), may hold values from 0.2 to 1
- parent_blocks: int32 [8, 13], P('leaf'), may hold values from 0 to 15, as said below
Outputs:
- leaf_fronts: float32 [8, 4096, 4096], P('leaf', None, 'front')
- merged_fronts: float32 [8, 4096, 4096], P('leaf', None, 'front')
The draws below stay inside these ranges and needn't reach their ends.
Inputs may be any that keep to these rules, and one draw needn't show every extreme that they name: `tiles`: together with diag, every orig[l,g] is symmetric positive definite. `tile_pos`: every tile's row index is at least its column index. On one device and level, counting both indices of each tile (a diagonal tile twice), every tile index occurs either not at all or exactly 3 times; one index, the same on every device and level, occurs on every device. `parent_blocks`: each row is strictly increasing, begins with 0 and ends with 15.
All inputs are finite; a program needn't handle non-finite values.
Results may differ from the reference program's by a relative error of at most 0.0003.
Values may be sent and summed in bfloat16 or wider, within the bound.
A program may use at most 192 MiB of HBM per device.

```python
import jax
import jax.numpy as jnp
from jax import lax

F = 4096
B = 256
TB = 128
MOST = 3
LEVELS = 2
PIV = 768
UB = 13
NBLK = 16
NTC = 32
TILE_DEV = 24
N_LEAF = 8
N_FRONT = 16


def tile_layout(key):
    layout_count = LEVELS * N_LEAF * N_FRONT
    group_count = TILE_DEV // 3
    shared_index = jax.random.randint(jax.random.fold_in(key, 3), (), 0, NTC)
    device_keys = jax.random.split(jax.random.fold_in(key, 5), layout_count)

    def one_device(device_key):
        order_key, shuffle_key = jax.random.split(device_key)
        head_zero = jnp.zeros((1,), jnp.int32)
        order = (jnp.concatenate([head_zero, 1 + jax.random.permutation(order_key, NTC - 1).astype(jnp.int32)]) + shared_index) % NTC
        first_index = order[:group_count].astype(jnp.int32)
        second_index = order[group_count:2 * group_count].astype(jnp.int32)
        shuffle = jax.random.permutation(shuffle_key, TILE_DEV).astype(jnp.int32)
        return (first_index, second_index, shuffle)
    return jax.vmap(one_device)(device_keys)


def draw_tile_pos(key, part):
    first_all, second_all, shuffle_all = tile_layout(key)

    def one_device(first_index, second_index, shuffle):
        tile_rows = jnp.concatenate([first_index, second_index, jnp.maximum(first_index, second_index)])
        tile_cols = jnp.concatenate([first_index, second_index, jnp.minimum(first_index, second_index)])
        return jnp.stack([tile_rows[shuffle], tile_cols[shuffle]]).astype(jnp.int32)
    placed = jax.vmap(one_device)(first_all, second_all, shuffle_all)
    return placed.reshape(LEVELS, N_LEAF, N_FRONT, 2, TILE_DEV).astype(jnp.int32)


def draw_tiles(key, part):
    first_all, second_all, shuffle_all = tile_layout(key)
    key = jax.random.fold_in(key, 11)
    device_keys = jax.random.split(key, LEVELS * N_LEAF * N_FRONT)
    group_count = TILE_DEV // 3
    residual_count = 2 * TB

    def one_device(inputs):
        device_key, first_index, second_index, shuffle = inputs
        value_key = jax.random.fold_in(device_key, 0)
        noise = jax.random.uniform(value_key, (group_count, residual_count, 2, TB), jnp.float32, -1.0, 1.0)
        jacobian = 3.0 * noise
        first_part = jacobian[:, :, 0, :]
        second_part = jacobian[:, :, 1, :]
        diag_first = 0.5 * jnp.einsum('gka,gkb->gab', first_part, first_part, precision=lax.Precision.HIGHEST)
        diag_second = 0.5 * jnp.einsum('gka,gkb->gab', second_part, second_part, precision=lax.Precision.HIGHEST)
        cross = jnp.einsum('gka,gkb->gab', first_part, second_part, precision=lax.Precision.HIGHEST)
        lower_cross = jnp.where((first_index > second_index)[:, None, None], cross, jnp.swapaxes(cross, 1, 2))
        every_tile = jnp.concatenate([diag_first, diag_second, lower_cross], axis=0)
        return every_tile[shuffle].astype(jnp.bfloat16)
    drawn = lax.map(one_device, (device_keys, first_all, second_all, shuffle_all))
    return drawn.reshape(LEVELS, N_LEAF, N_FRONT, TILE_DEV, TB, TB)


def draw_parent_blocks(key, part):
    group_keys = jax.random.split(jax.random.fold_in(key, 9), N_LEAF)

    def one_group(group_key):
        shuffled = jax.random.permutation(group_key, NBLK - 2)
        middle_blocks = jnp.argsort((shuffled >= UB - 2).astype(jnp.int32), stable=True)[:UB - 2] + 1
        first_block = jnp.zeros((1,), jnp.int32)
        last_block = jnp.full((1,), NBLK - 1, jnp.int32)
        return jnp.concatenate([first_block, middle_blocks.astype(jnp.int32), last_block]).astype(jnp.int32)
    return jax.vmap(one_group)(group_keys)


def shard_levels(key, dims, cuts, smallest, largest):
    def one(position, blocks):
        heights = jax.random.uniform(jax.random.fold_in(jax.random.fold_in(key, 6), position), (blocks,), jnp.float32, smallest / len(cuts), largest / len(cuts))
        return jnp.repeat(jnp.exp(heights), dims[position] // blocks).reshape((-1,) + (1,) * (len(dims) - position - 1))

    gain = one(*cuts[0])
    for cut in cuts[1:]:
        gain = gain * one(*cut)
    return gain


def setup_inputs(seed: int = 0) -> dict:
    keys = jax.random.split(jax.random.key(seed), 5)
    tiles = draw_tiles(jax.random.fold_in(keys[4], 71), 0)
    tile_pos = draw_tile_pos(jax.random.fold_in(keys[4], 71), 0)
    diag = jnp.clip(0.2 + 0.8 * jax.random.uniform(keys[2], (LEVELS, N_LEAF, F), jnp.float32) ** shard_levels(keys[2], (LEVELS, N_LEAF, F), ((1, 8), (2, 16)), -0.2, 0.2), 0.2, 1.0)
    parent_blocks = draw_parent_blocks(jax.random.fold_in(keys[4], 71), 0)
    return dict(tiles=tiles, tile_pos=tile_pos, diag=diag, parent_blocks=parent_blocks)


def assemble(diag_row, level_tiles, positions):
    tile_rows = positions[:, 0, :].reshape(-1)
    tile_cols = positions[:, 1, :].reshape(-1)
    tile_values = level_tiles.reshape(-1, TB, TB).astype(jnp.float32)
    blocked = jnp.zeros((NTC, TB, NTC, TB), jnp.float32).at[tile_rows, :, tile_cols, :].add(tile_values)
    hessian = blocked.reshape(F, F)
    weight_scale = 1.0 / (MOST * N_FRONT * TB)
    return weight_scale * (hessian + hessian.T) + jnp.diag(diag_row)

def factor_panels(front):
    pivot_block = front[:PIV, :PIV]
    below_block = front[PIV:, :PIV]
    update_block = front[PIV:, PIV:]
    diag_factor = jnp.linalg.cholesky(pivot_block)
    below_factor = lax.linalg.triangular_solve(diag_factor, below_block, left_side=False, lower=True, transpose_a=True)
    schur_block = update_block - jnp.dot(below_factor, below_factor.T, precision=lax.Precision.HIGHEST)
    factored = jnp.zeros((F, F), jnp.float32)
    factored = factored.at[:PIV, :PIV].set(jnp.tril(diag_factor))
    factored = factored.at[PIV:, :PIV].set(below_factor)
    factored = factored.at[PIV:, PIV:].set(jnp.tril(schur_block))
    return (factored, schur_block)

def extend(schur_block, blocks):
    parent_rows = (blocks[:, None] * B + jnp.arange(B, dtype=jnp.int32)[None, :]).reshape(-1)
    return jnp.zeros((F, F), jnp.float32).at[parent_rows[:, None], parent_rows[None, :]].set(schur_block)

def reference(tiles, tile_pos, diag, parent_blocks):
    leaf_list = []
    contributions = []
    for group_index in range(N_LEAF):
        front = assemble(diag[0, group_index], tiles[0, group_index], tile_pos[0, group_index])
        factored, schur_block = factor_panels(front)
        leaf_list.append(factored)
        own_part = assemble(diag[1, group_index], tiles[1, group_index], tile_pos[1, group_index])
        contributions.append(own_part + extend(schur_block, parent_blocks[group_index]))
    merged_list = []
    for pair_index in range(N_LEAF // 2):
        factored, unused_schur = factor_panels(contributions[2 * pair_index] + contributions[2 * pair_index + 1])
        merged_list.append(factored)
        merged_list.append(factored)
    return (jnp.stack(leaf_list), jnp.stack(merged_list))
```

```python
import functools

import jax
import jax.numpy as jnp
from jax import lax
from jax.experimental import pallas as pl
from jax.experimental.pallas import tpu as pltpu
from jax.sharding import PartitionSpec as P

F = 4096
B = 256
TB = 128
PIV = 768
UB = 13
T = 24
NF = 16
SCALE = 1.0 / 6144.0
MESH = pl.DeviceIdType.MESH
HI = lax.Precision.HIGHEST
f32 = jnp.float32
bf16 = jnp.bfloat16
VM = pl.BlockSpec(memory_space=pltpu.VMEM)
SM = pl.BlockSpec(memory_space=pltpu.SMEM)
LIMIT = 56 << 20
WIDTH = 8


def params(**more):
    return pltpu.CompilerParams(vmem_limit_bytes=LIMIT, **more)


def f32s(*shape):
    return jax.ShapeDtypeStruct(shape, f32)


def dot(a, b, ca, cb):
    return lax.dot_general(
        a, b, (((ca,), (cb,)), ((), ())), precision=HI, preferred_element_type=f32
    )


def row_col(pos, level, src, t):
    base = (level * NF + src) * 2 * T
    return pos[base + t], pos[base + T + t]


def lifted(pb, index):
    return 2 * pb[jnp.maximum(index - 6, 0) // 2] + lax.rem(index, 2)


def owner(r, c):
    return jnp.where(c >= 6, c, r)


def pack_kernel(pos, pb, tiles, slab, big0, bigm, cnt):
    me = lax.axis_index("front")

    def clear(i, _):
        cnt[i] = 0
        return 0

    lax.fori_loop(0, 64, clear, 0)

    def bump(i):
        old = cnt[i]
        cnt[i] = old + 1
        return old

    def put_slab(value, par, slot):
        for h in range(8):
            slab[par * 8 + h, slot] = value[16 * h : 16 * h + 16]

    def put_big(out, base, counter, r, c, tile, turned):
        dest = owner(r, c) // 2
        slot = bump(counter + dest) + base

        @pl.when(c >= 6)
        def _():
            out[dest, slot] = tile

        @pl.when(c < 6)
        def _():
            out[dest, slot] = turned

    def step(t, _):
        r, c = row_col(pos, 0, me, t)
        tile = tiles[0, t]
        turned = tile.astype(f32).T.astype(bf16)

        @pl.when(jnp.logical_and(c < 6, r < 12))
        def _():
            par = lax.rem(c, 2)
            put_slab(turned, par, bump(48 + par))

        @pl.when(r >= 6)
        def _():
            put_big(big0, 0, 0, r, c, tile, turned)

        @pl.when(c >= 6)
        def _():
            er, ec = lifted(pb, r), lifted(pb, c)

            @pl.when(er < 6)
            def _():
                par = lax.rem(ec, 2)
                put_slab(turned, par, 9 + bump(50 + par))

            @pl.when(er >= 6)
            def _():
                put_big(bigm, 0, 16, er, ec, tile, turned)

        r, c = row_col(pos, 1, me, t)
        tile1 = tiles[1, t]
        turned1 = tile1.astype(f32).T.astype(bf16)

        @pl.when(r < 6)
        def _():
            par = lax.rem(c, 2)
            put_slab(turned1, par, 18 + bump(52 + par))

        @pl.when(r >= 6)
        def _():
            put_big(bigm, 6, 32, r, c, tile1, turned1)

        return 0

    lax.fori_loop(0, T, step, 0)


def pack(pos, pb, tiles):
    return pl.pallas_call(
        pack_kernel,
        out_shape=[
            jax.ShapeDtypeStruct((NF, 27, 16, TB), bf16),
            jax.ShapeDtypeStruct((NF, 6, TB, TB), bf16),
            jax.ShapeDtypeStruct((NF, 12, TB, TB), bf16),
        ],
        in_specs=[SM, SM, VM],
        out_specs=[VM, VM, VM],
        scratch_shapes=[pltpu.SMEM((64,), jnp.int32)],
        compiler_params=params(),
        name="pack",
    )(pos, pb, tiles)


def slab_kernel(pos, pb, x, diag, out):
    me = lax.axis_index("front")
    mine = me // 8
    out[...] = jnp.zeros_like(out)
    for i in range(4):
        out[54, i : i + 1] = diag[i : i + 1]

    def source(s, _):
        def step(t, counts):
            na, ne, nl = counts
            r, c = row_col(pos, 0, s, t)
            hit_a = jnp.logical_and(jnp.logical_and(c < 6, r < 12), lax.rem(c, 2) == mine)

            @pl.when(hit_a)
            def _():
                at = (c // 2) * 18 + r
                out[at] = out[at] + SCALE * x[s, na].astype(f32)

            er, ec = lifted(pb, r), lifted(pb, c)
            hit_e = jnp.logical_and(jnp.logical_and(c >= 6, er < 6), lax.rem(ec, 2) == mine)

            @pl.when(hit_e)
            def _():
                at = (ec // 2) * 18 + 12 + er
                out[at] = out[at] + SCALE * x[s, 9 + ne].astype(f32)

            r1, c1 = row_col(pos, 1, s, t)
            hit_l = jnp.logical_and(r1 < 6, lax.rem(c1, 2) == mine)

            @pl.when(hit_l)
            def _():
                at = (c1 // 2) * 18 + 12 + r1
                out[at] = out[at] + SCALE * x[s, 18 + nl].astype(f32)

            add = lambda n, hit: n + jnp.where(hit, 1, 0)
            return add(na, hit_a), add(ne, hit_e), add(nl, hit_l)

        zero = jnp.int32(0)
        lax.fori_loop(0, T, step, (zero, zero, zero))
        return 0

    lax.fori_loop(0, NF, source, 0)


def slab_sum(pos, pb, x, diag):
    return pl.pallas_call(
        slab_kernel,
        out_shape=f32s(56, 16, TB),
        in_specs=[SM, SM, VM, VM],
        out_specs=VM,
        compiler_params=params(),
        name="slab",
    )(pos, pb, x, diag)


def eye_mask():
    return lax.broadcasted_iota(jnp.int32, (TB, TB), 0) == lax.broadcasted_iota(
        jnp.int32, (TB, TB), 1
    )


def place(up, low, r, c, value):
    col = pl.multiple_of(lax.rem(owner(r, c), 2) * TB, TB)

    @pl.when(c >= 6)
    def _():
        row = pl.multiple_of((r - 6) * TB, TB)
        low[pl.ds(row, TB), pl.ds(col, TB)] = low[pl.ds(row, TB), pl.ds(col, TB)] + value

        @pl.when(r == c)
        def _():
            low[pl.ds(row, TB), pl.ds(col, TB)] = low[pl.ds(row, TB), pl.ds(col, TB)] + value.T

    @pl.when(c < 6)
    def _():
        row = pl.multiple_of(c * TB, TB)
        up[pl.ds(row, TB), pl.ds(col, TB)] = up[pl.ds(row, TB), pl.ds(col, TB)] + value


def add_diag(low, me, row0, row1):
    @pl.when(me >= 3)
    def _():
        for half, row in enumerate((row0, row1)):
            at = pl.multiple_of((me - 3) * B + half * TB, TB)
            cols = slice(half * TB, half * TB + TB)
            low[pl.ds(at, TB), cols] = low[pl.ds(at, TB), cols] + jnp.where(
                eye_mask(), jnp.broadcast_to(row, (TB, TB)), 0.0
            )


def leaf_kernel(pos, x, diag, up, low):
    me = lax.axis_index("front")
    up[...] = jnp.zeros_like(up)
    low[...] = jnp.zeros_like(low)

    def source(s, _):
        def step(t, n):
            r, c = row_col(pos, 0, s, t)
            hit = jnp.logical_and(r >= 6, owner(r, c) // 2 == me)

            @pl.when(hit)
            def _():
                place(up, low, r, c, SCALE * x[s, n].astype(f32))

            return n + jnp.where(hit, 1, 0)

        lax.fori_loop(0, T, step, jnp.int32(0))
        return 0

    lax.fori_loop(0, NF, source, 0)
    add_diag(low, me, diag[0:1], diag[1:2])


def leaf_assemble(pos, x, diag):
    return pl.pallas_call(
        leaf_kernel,
        out_shape=[f32s(PIV, B), f32s(F - PIV, B)],
        in_specs=[SM, VM, VM],
        out_specs=[VM, VM],
        compiler_params=params(),
        name="leafasm",
    )(pos, x, diag)


def parent_kernel(pos, pb, x, slab, diag, up, low):
    me = lax.axis_index("front")
    up[...] = jnp.zeros_like(up)
    low[...] = jnp.zeros_like(low)

    def source(s, _):
        def step(t, counts):
            ne, nl = counts
            r, c = row_col(pos, 0, s, t)
            er, ec = lifted(pb, r), lifted(pb, c)
            hit_e = jnp.logical_and(
                jnp.logical_and(c >= 6, er >= 6), owner(er, ec) // 2 == me
            )

            @pl.when(hit_e)
            def _():
                place(up, low, er, ec, SCALE * x[s, ne].astype(f32))

            r1, c1 = row_col(pos, 1, s, t)
            hit_l = jnp.logical_and(r1 >= 6, owner(r1, c1) // 2 == me)

            @pl.when(hit_l)
            def _():
                place(up, low, r1, c1, SCALE * x[s, 6 + nl].astype(f32))

            return ne + jnp.where(hit_e, 1, 0), nl + jnp.where(hit_l, 1, 0)

        zero = jnp.int32(0)
        lax.fori_loop(0, T, step, (zero, zero))
        return 0

    lax.fori_loop(0, NF, source, 0)
    add_diag(low, me, diag[2:3], diag[3:4])

    def extended(u, _):
        @pl.when(pb[u] == me)
        def _():
            rows = slab[u + 3, 54]
            add_diag(low, me, rows[0:1], rows[1:2])

        return 0

    lax.fori_loop(0, UB, extended, 0)


def parent_assemble(pos, pb, x, slab, diag):
    return pl.pallas_call(
        parent_kernel,
        out_shape=[f32s(PIV, B), f32s(F - PIV, B)],
        in_specs=[SM, SM, VM, VM, VM],
        out_specs=[VM, VM],
        compiler_params=params(),
        name="parentasm",
    )(pos, pb, x, slab, diag)


def lanes(x, j):
    return jnp.broadcast_to(x[:, j : j + 1], (8, TB))


def rows8(x, i):
    return jnp.broadcast_to(x[i : i + 1, :], (8, TB))


def factor_block(block):
    w = WIDTH
    s_rows = list(block)
    sub = lax.broadcasted_iota(jnp.int32, (8, TB), 0)
    lane = lax.broadcasted_iota(jnp.int32, (8, TB), 1)
    inv_rows = [(lane == sub + 8 * v).astype(f32) for v in range(16)]
    for k0 in range(0, TB, w):
        v0, s = k0 // 8, k0 % 8
        m = {(v, j): lanes(s_rows[v], k0 + j) for v in range(v0, 16) for j in range(w)}
        p = {(i, j): rows8(m[v0, j], s + i) for j in range(w) for i in range(j, w)}
        r_rows = [rows8(s_rows[v0], s + i) for i in range(w)]
        q_rows = [rows8(inv_rows[v0], s + i) for i in range(w)]
        low, scale = {}, []
        for j in range(w):
            d = p[j, j]
            for t in range(j):
                d = d - low[j, t] * low[j, t]
            rs = lax.rsqrt(d)
            scale.append(rs)
            for i in range(j + 1, w):
                x = p[i, j]
                for t in range(j):
                    x = x - low[i, t] * low[j, t]
                low[i, j] = x * rs
        us, ws = [], []
        for i in range(w):
            x, q = r_rows[i], q_rows[i]
            for t in range(i):
                x = x - low[i, t] * us[t]
                q = q - low[i, t] * ws[t]
            us.append(x * scale[i])
            ws.append(q * scale[i])
        for v in range(v0, 16):
            cs = []
            for i in range(w):
                x = m[v, i]
                for t in range(i):
                    x = x - low[i, t] * cs[t]
                cs.append(x * scale[i])
            if v == v0:
                cs = [jnp.where(sub >= s + w, x, 0.0) for x in cs]
            a, b = s_rows[v], inv_rows[v]
            for i in range(w):
                a = a - cs[i] * us[i]
                b = b - cs[i] * ws[i]
            if v == v0:
                for i in range(w):
                    a = jnp.where(sub == s + i, us[i], a)
                    b = jnp.where(sub == s + i, ws[i], b)
            s_rows[v], inv_rows[v] = a, b
    s_rows = [jnp.where(lane >= sub + 8 * v, s_rows[v], 0.0) for v in range(16)]
    return s_rows, inv_rows


def factor(a, u, li, n):
    for k in range(6):
        o = k * TB
        r = o + TB
        us, inv = factor_block([a[o + 8 * v : o + 8 * v + 8, o:r] for v in range(16)])
        for v in range(16):
            u[o + 8 * v : o + 8 * v + 8, o:r] = us[v]
            li[o + 8 * v : o + 8 * v + 8, :] = inv[v]
        if r < n:
            u[o:r, r:n] = dot(li[o:r, :], a[o:r, r:n], 1, 0)
            for q in range(r, PIV, TB):
                a[q : q + TB, q:n] = a[q : q + TB, q:n] - dot(
                    u[o:r, q : q + TB], u[o:r, q:n], 0, 0
                )


def first_kernel(pb, slab, own, u11, xt, p11, a, u, li):
    n = 2 * PIV + B

    def unpack(d, _):
        for cb in range(3):
            row = pl.multiple_of((2 * cb + d // 8) * TB + 16 * lax.rem(d, 8), 16)
            for k in range(12):
                a[pl.ds(row, 16), k * TB : k * TB + TB] = slab[d, cb * 18 + k]
            for k in range(6):
                p11[pl.ds(row, 16), k * TB : k * TB + TB] = slab[d, cb * 18 + 12 + k]
        return 0

    lax.fori_loop(0, NF, unpack, 0)
    eye = eye_mask()
    for b in range(6):
        cut = slice(b * TB, b * TB + TB)
        for ref, at in ((a, 0), (p11, 2)):
            block = ref[cut, cut]
            row = slab[b // 2, 54][at + b % 2 : at + b % 2 + 1]
            ref[cut, cut] = block + block.T + jnp.where(eye, jnp.broadcast_to(row, (TB, TB)), 0.0)
    a[:, 2 * PIV : n] = own[...]
    factor(a, u, li, n)
    u11[...] = u[:, :PIV]
    for i in range(6):
        for j in range(2):
            xt[j * TB : j * TB + TB, i * TB : i * TB + TB] = u[
                i * TB : i * TB + TB, 2 * PIV + j * TB : 2 * PIV + j * TB + TB
            ].T
    for v in range(3):

        @pl.when(pb[v] < 3)
        def _():
            to_col = pl.multiple_of(pb[v] * B, B)
            for half in range(2):
                at = pl.multiple_of(pb[v] * B + half * TB, TB)
                row = slab[v + 3, 54][half : half + 1]
                p11[pl.ds(at, TB), pl.ds(at, TB)] = p11[pl.ds(at, TB), pl.ds(at, TB)] + jnp.where(
                    eye, jnp.broadcast_to(row, (TB, TB)), 0.0
                )
            for w in range(v + 1):
                to_row = pl.multiple_of(pb[w] * B, B)
                gram = dot(
                    u[:, PIV + w * B : PIV + w * B + B], u[:, PIV + v * B : PIV + v * B + B], 0, 0
                )
                p11[pl.ds(to_row, B), pl.ds(to_col, B)] = (
                    p11[pl.ds(to_row, B), pl.ds(to_col, B)] - gram
                )


def first_factor(pb, slab, own):
    n = 2 * PIV + B
    return pl.pallas_call(
        first_kernel,
        out_shape=[f32s(PIV, PIV), f32s(B, PIV), f32s(PIV, PIV)],
        in_specs=[SM, VM, VM],
        out_specs=[VM, VM, VM],
        scratch_shapes=[
            pltpu.VMEM((PIV, n), f32),
            pltpu.VMEM((PIV, n), f32),
            pltpu.VMEM((PIV, TB), f32),
        ],
        compiler_params=params(),
        cost_estimate=pl.CostEstimate(
            flops=30_000_000_000, bytes_accessed=100_000_000, transcendentals=0
        ),
        name="first",
    )(pb, slab, own)


def second_kernel(own, other, u, li, a):
    a[...] = own[...] + other[...]
    factor(a, u, li, PIV)


def second_factor(own, other):
    return pl.pallas_call(
        second_kernel,
        out_shape=[f32s(PIV, PIV), f32s(PIV, TB)],
        in_specs=[VM, VM],
        out_specs=[VM, VM],
        scratch_shapes=[pltpu.VMEM((PIV, PIV), f32)],
        compiler_params=params(),
        cost_estimate=pl.CostEstimate(
            flops=20_000_000_000, bytes_accessed=100_000_000, transcendentals=0
        ),
        name="second",
    )(own, other)


def solve_kernel(u, li, own, other, xt, a):
    a[...] = own[...] + other[...]
    for k in range(6):
        o, r = k * TB, k * TB + TB
        x = dot(li[o:r, :], a[o:r, :], 1, 0)
        for j in range(2):
            xt[j * TB : j * TB + TB, o:r] = x[:, j * TB : j * TB + TB].T
        if r < PIV:
            a[r:, :] = a[r:, :] - dot(u[o:r, r:], x, 0, 0)


def solve(u, li, own, other):
    return pl.pallas_call(
        solve_kernel,
        out_shape=f32s(B, PIV),
        in_specs=[VM] * 4,
        out_specs=VM,
        scratch_shapes=[pltpu.VMEM((PIV, B), f32)],
        compiler_params=params(),
        name="solve",
    )(u, li, own, other)


def write_front(me, xall, u11, low, out):
    sub = lax.broadcasted_iota(jnp.int32, (B, B), 0)
    lane = lax.broadcasted_iota(jnp.int32, (B, B), 1)

    @pl.when(me >= 3)
    def _():
        def clear(k, _):
            out[pl.ds(pl.multiple_of(k * B, B), B), :] = jnp.zeros((B, B), f32)
            return 0

        lax.fori_loop(0, me, clear, 0)

        def update(k, _):
            at = pl.ds(pl.multiple_of((k - 3) * B, B), B)
            value = low(at) - dot(xall[k], xall[me], 1, 1)
            value = jnp.where(jnp.logical_or(k > me, sub >= lane), value, 0.0)
            out[pl.ds(pl.multiple_of(k * B, B), B), :] = value
            return 0

        lax.fori_loop(me, NF, update, 0)

    @pl.when(me < 3)
    def _():
        cols = pl.ds(pl.multiple_of(me * B, B), B)

        def copy(k, _):
            out[pl.ds(pl.multiple_of(k * B, B), B), :] = xall[k, :, cols]
            return 0

        lax.fori_loop(3, NF, copy, 0)
        for ib in range(6):
            for half in range(2):
                jb = 2 * me + half
                src = u11[pl.ds(pl.multiple_of(jb * TB, TB), TB), ib * TB : ib * TB + TB].T
                out[ib * TB : ib * TB + TB, half * TB : half * TB + TB] = jnp.where(
                    ib >= jb, src, 0.0
                )


def leaf_out_kernel(pb, xall, u11, alow, cup, clow, out, vup, vlow):
    me = lax.axis_index("front")
    vup[...] = cup[...]
    vlow[...] = clow[...]
    write_front(me, xall, u11, lambda at: alow[at, :], out)

    def column(v, _):
        @pl.when(jnp.logical_and(pb[v] == me, me >= 3))
        def _():
            def row(w, _):
                q = pb[w]

                @pl.when(q < 3)
                def _():
                    at = pl.ds(pl.multiple_of(q * B, B), B)
                    vup[at, :] = vup[at, :] - dot(xall[w + 3], xall[v + 3], 1, 1)

                @pl.when(q >= me)
                def _():
                    at = pl.ds(pl.multiple_of((q - 3) * B, B), B)
                    vlow[at, :] = vlow[at, :] - dot(xall[w + 3], xall[v + 3], 1, 1)

                return 0

            lax.fori_loop(0, UB, row, 0)

        return 0

    lax.fori_loop(0, UB, column, 0)


def leaf_output(pb, xall, u11, alow, cup, clow):
    return pl.pallas_call(
        leaf_out_kernel,
        out_shape=[f32s(F, B), f32s(PIV, B), f32s(F - PIV, B)],
        in_specs=[SM] + [VM] * 5,
        out_specs=[VM] * 3,
        compiler_params=params(),
        name="leafout",
    )(pb, xall, u11, alow, cup, clow)


def merged_out_kernel(xown, xother, u11, low0, low1, out, xall):
    me = lax.axis_index("front")
    core = lax.rem(lax.axis_index("leaf"), 2)
    mine = pl.ds(pl.multiple_of(core * TB, TB), TB)
    theirs = pl.ds(pl.multiple_of(TB - core * TB, TB), TB)

    def join(k, _):
        xall[k, mine, :] = xown[k]
        xall[k, theirs, :] = xother[k]
        return 0

    lax.fori_loop(3, NF, join, 0)
    write_front(me, xall, u11, lambda at: low0[at, :] + low1[at, :], out)


def merged_output(xown, xother, u11, low0, low1):
    return pl.pallas_call(
        merged_out_kernel,
        out_shape=f32s(F, B),
        in_specs=[VM] * 5,
        out_specs=VM,
        scratch_shapes=[pltpu.VMEM((NF, B, PIV), f32)],
        compiler_params=params(),
        name="mergedout",
    )(xown, xother, u11, low0, low1)


def gather_kernel(x, out, ss, rs, ls):
    me = lax.axis_index("front")
    y, z = me // 4, lax.rem(me, 4)

    def at(yy, zz):
        return lax.rem(yy + 8, 4) * 4 + lax.rem(zz + 8, 4)

    zr, zl, yr, yl = at(y, z + 1), at(y, z - 1), at(y + 1, z), at(y - 1, z)
    gate = pltpu.get_barrier_semaphore()
    for peer in (zr, zl, yr, yl):
        pl.semaphore_signal(gate, inc=1, device_id={"front": peer}, device_id_type=MESH)
    pl.semaphore_wait(gate, 4)
    half = x.shape[0] // 2
    part = half // 2
    own = pltpu.make_async_copy(x, out.at[me], ls)
    own.start()
    copies = []

    def send(src, dst, peer):
        i = len(copies)
        copy = pltpu.make_async_remote_copy(
            src_ref=src,
            dst_ref=dst,
            send_sem=ss.at[i],
            recv_sem=rs.at[i],
            device_id={"front": peer},
            device_id_type=MESH,
        )
        copy.start()
        copies.append(copy)
        return copy

    a, b = pl.ds(0, half), pl.ds(half, half)
    a0, a1 = pl.ds(0, part), pl.ds(part, part)
    b0, b1 = pl.ds(half, part), pl.ds(half + part, part)

    def pass_on(block, rows, peer):
        return send(out.at[block, rows], out.at[block, rows], peer)

    a1r = send(x.at[a], out.at[me, a], zr)
    a1l = send(x.at[a], out.at[me, a], zl)
    b1r = send(x.at[b], out.at[me, b], yr)
    b1l = send(x.at[b], out.at[me, b], yl)
    a1r.wait_recv()
    a2r = pass_on(zl, a0, zr)
    a1l.wait_recv()
    a2l = pass_on(zr, a1, zl)
    b1r.wait_recv()
    b2r = pass_on(yl, b0, yr)
    b1l.wait_recv()
    b2l = pass_on(yr, b1, yl)
    own.wait()
    zo, yo = at(y, z + 2), at(y + 2, z)
    ar, al, br, bl = [], [], [], []

    def second(block_a, block_b):
        ar.append(pass_on(block_a, a, yr))
        al.append(pass_on(block_a, a, yl))
        br.append(pass_on(block_b, b, zr))
        bl.append(pass_on(block_b, b, zl))

    second(me, me)
    second(zl, yl)
    second(zr, yr)
    for copy in (a2r, a2l, b2r, b2l):
        copy.wait_recv()
    second(zo, yo)
    last = []
    for q, o in enumerate((0, -1, 1, 2)):
        ar[q].wait_recv()
        last.append(pass_on(at(y - 1, z + o), a0, yr))
        al[q].wait_recv()
        last.append(pass_on(at(y + 1, z + o), a1, yl))
        br[q].wait_recv()
        last.append(pass_on(at(y + o, z - 1), b0, zr))
        bl[q].wait_recv()
        last.append(pass_on(at(y + o, z + 1), b1, zl))
    for copy in last:
        copy.wait_recv()
    for copy in copies:
        copy.wait_send()


def gather(x, number):
    return pl.pallas_call(
        gather_kernel,
        out_shape=jax.ShapeDtypeStruct((NF,) + x.shape, x.dtype),
        in_specs=[VM],
        out_specs=VM,
        scratch_shapes=[
            pltpu.SemaphoreType.DMA((40,)),
            pltpu.SemaphoreType.DMA((40,)),
            pltpu.SemaphoreType.DMA,
        ],
        compiler_params=params(collective_id=number, has_side_effects=True),
        name="gather%d" % number,
    )(x)


def exchange(x):
    route = [(i, i ^ 1) for i in range(lax.axis_size("leaf"))]
    return jax.tree.map(lambda v: lax.ppermute(v, "leaf", route), x)


def body(tiles, tile_pos, diag, parent_blocks):
    pos = tile_pos.reshape(-1)
    pb = parent_blocks.reshape(-1)
    diag = diag.reshape(4, TB)
    slab, big0, bigm = pack(pos, pb, tiles.reshape(2, T, TB, TB))
    to_all = lambda x: lax.all_to_all(x, "front", 0, 0, tiled=True)
    slab = slab_sum(pos, pb, to_all(slab), diag)
    slab = gather(slab.reshape(56 * 16, TB), 1).reshape(NF, 56, 16, TB)
    aup, alow = leaf_assemble(pos, to_all(big0), diag)
    u11, xt, p11 = first_factor(pb, slab, aup)
    xall = lax.all_gather(xt, "front")
    cup, clow = parent_assemble(pos, pb, to_all(bigm), slab, diag)
    m_u11, m_li = second_factor(p11, exchange(p11))
    leaf, vup, vlow = leaf_output(pb, xall, u11, alow, cup, clow)
    sup, slow = exchange((vup, vlow))
    m_xt = solve(m_u11, m_li, vup, sup)
    core = lax.rem(lax.axis_index("leaf"), 2)
    m_half = gather(lax.dynamic_slice_in_dim(m_xt, core * TB, TB, 0), 2)
    merged = merged_output(m_half, exchange(m_half), m_u11, vlow, slow)
    return leaf[None], merged[None]


def solution(mesh):
    placed = (
        P(None, "leaf", "front", None, None, None),
        P(None, "leaf", None, None, None),
        P(None, "leaf", "front"),
        P("leaf", None),
    )
    return jax.shard_map(
        body,
        mesh=mesh,
        in_specs=placed,
        out_specs=(P("leaf", None, "front"), P("leaf", None, "front")),
        check_vma=False,
    )
```

```python
import functools

import jax
import jax.numpy as jnp
from jax import lax
from jax.experimental import pallas as pl
from jax.experimental.pallas import tpu as pltpu
from jax.sharding import PartitionSpec as P

F = 4096
B = 256
TB = 128
PIV = 768
UB = 13
T = 24
NF = 16
SCALE = 1.0 / 6144.0
MESH = pl.DeviceIdType.MESH
HI = lax.Precision.HIGHEST
f32 = jnp.float32
bf16 = jnp.bfloat16
VM = pl.BlockSpec(memory_space=pltpu.VMEM)
SM = pl.BlockSpec(memory_space=pltpu.SMEM)
ANY = pl.BlockSpec(memory_space=pl.ANY)
LIMIT = 56 << 20
WIDTH = 8


def params(**more):
    return pltpu.CompilerParams(vmem_limit_bytes=LIMIT, **more)


def f32s(*shape):
    return jax.ShapeDtypeStruct(shape, f32)


def dot(a, b, ca, cb):
    return lax.dot_general(
        a, b, (((ca,), (cb,)), ((), ())), precision=HI, preferred_element_type=f32
    )


def row_col(pos, level, src, t):
    base = (level * NF + src) * 2 * T
    return pos[base + t], pos[base + T + t]


def lifted(pb, index):
    return 2 * pb[jnp.maximum(index - 6, 0) // 2] + lax.rem(index, 2)


def owner(r, c):
    return jnp.where(c >= 6, c, r)


def pack_kernel(pos, pb, tiles, slab, big0, bigm, cnt):
    me = lax.axis_index("front")

    def clear(i, _):
        cnt[i] = 0
        return 0

    lax.fori_loop(0, 64, clear, 0)

    def bump(i):
        old = cnt[i]
        cnt[i] = old + 1
        return old

    def put_slab(value, par, slot):
        for h in range(8):
            slab[par * 8 + h, slot] = value[16 * h : 16 * h + 16]

    def put_big(out, base, counter, r, c, tile, turned):
        dest = owner(r, c) // 2
        slot = bump(counter + dest) + base

        @pl.when(c >= 6)
        def _():
            out[dest, slot] = tile

        @pl.when(c < 6)
        def _():
            out[dest, slot] = turned

    def step(t, _):
        r, c = row_col(pos, 0, me, t)
        tile = tiles[0, t]
        turned = tile.astype(f32).T.astype(bf16)

        @pl.when(jnp.logical_and(c < 6, r < 12))
        def _():
            par = lax.rem(c, 2)
            put_slab(turned, par, bump(48 + par))

        @pl.when(r >= 6)
        def _():
            put_big(big0, 0, 0, r, c, tile, turned)

        @pl.when(c >= 6)
        def _():
            er, ec = lifted(pb, r), lifted(pb, c)

            @pl.when(er < 6)
            def _():
                par = lax.rem(ec, 2)
                put_slab(turned, par, 9 + bump(50 + par))

            @pl.when(er >= 6)
            def _():
                put_big(bigm, 0, 16, er, ec, tile, turned)

        r, c = row_col(pos, 1, me, t)
        tile1 = tiles[1, t]
        turned1 = tile1.astype(f32).T.astype(bf16)

        @pl.when(r < 6)
        def _():
            par = lax.rem(c, 2)
            put_slab(turned1, par, 18 + bump(52 + par))

        @pl.when(r >= 6)
        def _():
            put_big(bigm, 6, 32, r, c, tile1, turned1)

        return 0

    lax.fori_loop(0, T, step, 0)


def pack(pos, pb, tiles):
    return pl.pallas_call(
        pack_kernel,
        out_shape=[
            jax.ShapeDtypeStruct((NF, 27, 16, TB), bf16),
            jax.ShapeDtypeStruct((NF, 6, TB, TB), bf16),
            jax.ShapeDtypeStruct((NF, 12, TB, TB), bf16),
        ],
        in_specs=[SM, SM, VM],
        out_specs=[VM, VM, VM],
        scratch_shapes=[pltpu.SMEM((64,), jnp.int32)],
        compiler_params=params(),
        name="pack",
    )(pos, pb, tiles)


def plan_kernel(pb, pos, out):
    me = lax.axis_index("front")
    half = me // 8
    r0, c0, r1, c1 = pos[0, 0], pos[0, 1], pos[1, 0], pos[1, 1]

    def lift(x):
        block = jnp.maximum(x - 6, 0) // 2
        to = jnp.zeros_like(x)
        for u in range(UB):
            to = jnp.where(block == u, pb[u], to)
        return 2 * to + lax.rem(x, 2)

    er, ec = lift(r0), lift(c0)

    def slab_code(c, r, start, slope):
        cb = c // 2
        return start + r + slope * cb - cb * cb

    def own_code(r, c):
        row = jnp.where(c >= 6, r, c)
        return 4 * row + 2 * lax.rem(owner(r, c), 2) + jnp.where(r == c, 1, 0)

    def own_hit(r, c):
        return (r >= 6) & (owner(r, c) // 2 == me)

    sets = (
        ((c0 < 6) & (r0 < 12) & (lax.rem(c0, 2) == half), slab_code(c0, r0, 0, 11)),
        ((c0 >= 6) & (er < 6) & (lax.rem(ec, 2) == half), slab_code(ec, er, 30, 5)),
        ((r1 < 6) & (lax.rem(c1, 2) == half), slab_code(c1, r1, 30, 5)),
        (own_hit(r0, c0), own_code(r0, c0)),
        ((c0 >= 6) & own_hit(er, ec), own_code(er, ec)),
        (own_hit(r1, c1), own_code(r1, c1)),
    )
    before = lax.broadcasted_iota(jnp.int32, (T, T), 0) < lax.broadcasted_iota(
        jnp.int32, (T, T), 1
    )
    before = before.astype(f32)
    lane = lax.broadcasted_iota(jnp.int32, (NF, TB), 1)
    for i, (hit, code) in enumerate(sets):
        one = jnp.where(hit, 1.0, 0.0)
        rank = dot(one, before, 1, 0)
        code = code.astype(f32)
        table = jnp.where(lane == TB - 1, jnp.sum(one, axis=1, keepdims=True), 0.0)
        for k in range(9):
            pick = jnp.where(rank == k, one * code, 0.0)
            table = jnp.where(lane == k, jnp.sum(pick, axis=1, keepdims=True), table)
        out[NF * i : NF * i + NF, :] = (table + 0.5).astype(jnp.int32)


def make_plan(pb, pos):
    return pl.pallas_call(
        plan_kernel,
        out_shape=jax.ShapeDtypeStruct((6 * NF, TB), jnp.int32),
        in_specs=[SM, VM],
        out_specs=VM,
        compiler_params=params(),
        name="plan",
    )(pb, pos)


def slab_kernel(plan, x, diag, out):
    out[...] = jnp.zeros_like(out)
    for i in range(4):
        out[42, i : i + 1] = diag[i : i + 1]

    def source(s, _):
        for i in range(3):

            def add(k, _, i=i):
                at = plan[i * NF + s, k]
                out[at] = out[at] + SCALE * x[s, 9 * i + k].astype(f32)
                return 0

            lax.fori_loop(0, plan[i * NF + s, TB - 1], add, 0)
        return 0

    lax.fori_loop(0, NF, source, 0)


def slab_sum(plan, x, diag):
    return pl.pallas_call(
        slab_kernel,
        out_shape=f32s(44, 16, TB),
        in_specs=[SM, VM, VM],
        out_specs=VM,
        compiler_params=params(),
        name="slab",
    )(plan, x, diag)


def eye_mask():
    return lax.broadcasted_iota(jnp.int32, (TB, TB), 0) == lax.broadcasted_iota(
        jnp.int32, (TB, TB), 1
    )


def place(up, low, code, value):
    row = code // 4
    col = pl.ds(pl.multiple_of(lax.rem(code // 2, 2) * TB, TB), TB)

    @pl.when(row >= 6)
    def _():
        at = pl.ds(pl.multiple_of((row - 6) * TB, TB), TB)
        low[at, col] = low[at, col] + value

        @pl.when(lax.rem(code, 2) == 1)
        def _():
            low[at, col] = low[at, col] + value.T

    @pl.when(row < 6)
    def _():
        at = pl.ds(pl.multiple_of(row * TB, TB), TB)
        up[at, col] = up[at, col] + value


def add_diag(low, me, row0, row1):
    @pl.when(me >= 3)
    def _():
        for half, row in enumerate((row0, row1)):
            at = pl.multiple_of((me - 3) * B + half * TB, TB)
            cols = slice(half * TB, half * TB + TB)
            low[pl.ds(at, TB), cols] = low[pl.ds(at, TB), cols] + jnp.where(
                eye_mask(), jnp.broadcast_to(row, (TB, TB)), 0.0
            )


def gather_tiles(plan, x, up, low, sets):
    first = sets[0]
    up[...] = jnp.zeros_like(up)
    low[...] = jnp.zeros_like(low)

    def source(s, _):
        for i in sets:

            def add(k, _, i=i):
                place(up, low, plan[i * NF + s, k], SCALE * x[s, 6 * (i - first) + k].astype(f32))
                return 0

            lax.fori_loop(0, plan[i * NF + s, TB - 1], add, 0)
        return 0

    lax.fori_loop(0, NF, source, 0)


def leaf_kernel(plan, x, diag, after, up, low):
    me = lax.axis_index("front")
    gather_tiles(plan, x, up, low, (3,))
    add_diag(low, me, diag[0:1], diag[1:2])


def leaf_assemble(plan, x, diag, after):
    return pl.pallas_call(
        leaf_kernel,
        out_shape=[f32s(PIV, B), f32s(F - PIV, B)],
        in_specs=[SM, VM, VM, ANY],
        out_specs=[VM, VM],
        compiler_params=params(),
        name="leafasm",
    )(plan, x, diag, after)


def parent_kernel(plan, pb, x, extra, diag, after, up, low):
    me = lax.axis_index("front")
    gather_tiles(plan, x, up, low, (4, 5))
    add_diag(low, me, diag[2:3], diag[3:4])

    def extended(u, _):
        @pl.when(pb[u] == me)
        def _():
            rows = extra[u + 3]
            add_diag(low, me, rows[0:1], rows[1:2])

        return 0

    lax.fori_loop(0, UB, extended, 0)


def parent_assemble(plan, pb, x, extra, diag, after):
    return pl.pallas_call(
        parent_kernel,
        out_shape=[f32s(PIV, B), f32s(F - PIV, B)],
        in_specs=[SM, SM, VM, VM, VM, ANY],
        out_specs=[VM, VM],
        compiler_params=params(),
        name="parentasm",
    )(plan, pb, x, extra, diag, after)


def lanes(x, j):
    return jnp.broadcast_to(x[:, j : j + 1], (8, TB))


def rows8(x, i):
    return jnp.broadcast_to(x[i : i + 1, :], (8, TB))


def factor_block(block):
    w = WIDTH
    s_rows = list(block)
    sub = lax.broadcasted_iota(jnp.int32, (8, TB), 0)
    lane = lax.broadcasted_iota(jnp.int32, (8, TB), 1)
    inv_rows = [(lane == sub + 8 * v).astype(f32) for v in range(16)]
    for k0 in range(0, TB, w):
        v0, s = k0 // 8, k0 % 8
        m = {(v, j): lanes(s_rows[v], k0 + j) for v in range(v0, 16) for j in range(w)}
        p = {(i, j): rows8(m[v0, j], s + i) for j in range(w) for i in range(j, w)}
        r_rows = [rows8(s_rows[v0], s + i) for i in range(w)]
        q_rows = [rows8(inv_rows[v0], s + i) for i in range(w)]
        low, scale = {}, []
        for j in range(w):
            d = p[j, j]
            for t in range(j):
                d = d - low[j, t] * low[j, t]
            rs = lax.rsqrt(d)
            scale.append(rs)
            for i in range(j + 1, w):
                x = p[i, j]
                for t in range(j):
                    x = x - low[i, t] * low[j, t]
                low[i, j] = x * rs
        us, ws = [], []
        for i in range(w):
            x, q = r_rows[i], q_rows[i]
            for t in range(i):
                x = x - low[i, t] * us[t]
                q = q - low[i, t] * ws[t]
            us.append(x * scale[i])
            ws.append(q * scale[i])
        for v in range(v0, 16):
            cs = []
            for i in range(w):
                x = m[v, i]
                for t in range(i):
                    x = x - low[i, t] * cs[t]
                cs.append(x * scale[i])
            if v == v0:
                cs = [jnp.where(sub >= s + w, x, 0.0) for x in cs]
            a, b = s_rows[v], inv_rows[v]
            for i in range(w):
                a = a - cs[i] * us[i]
                b = b - cs[i] * ws[i]
            if v == v0:
                for i in range(w):
                    a = jnp.where(sub == s + i, us[i], a)
                    b = jnp.where(sub == s + i, ws[i], b)
            s_rows[v], inv_rows[v] = a, b
    s_rows = [jnp.where(lane >= sub + 8 * v, s_rows[v], 0.0) for v in range(16)]
    return s_rows, inv_rows


def factor(a, u, li, n):
    for k in range(6):
        o = k * TB
        r = o + TB
        us, inv = factor_block([a[o + 8 * v : o + 8 * v + 8, o:r] for v in range(16)])
        for v in range(16):
            u[o + 8 * v : o + 8 * v + 8, o:r] = us[v]
            li[o + 8 * v : o + 8 * v + 8, :] = inv[v]
        if r < n:
            u[o:r, r:n] = dot(li[o:r, :], a[o:r, r:n], 1, 0)
            for q in range(r, PIV, TB):
                a[q : q + TB, q:n] = a[q : q + TB, q:n] - dot(
                    u[o:r, q : q + TB], u[o:r, q:n], 0, 0
                )


def first_kernel(pb, slab, after, u11, p11, li, a, u):
    n = 2 * PIV
    p11[...] = jnp.zeros_like(p11)

    def unpack(d, _):
        for cb in range(3):
            row = pl.multiple_of((2 * cb + d // 8) * TB + 16 * lax.rem(d, 8), 16)
            for k in range(2 * cb, 12):
                a[pl.ds(row, 16), k * TB : k * TB + TB] = slab[d, 11 * cb - cb * cb + k]
            for k in range(2 * cb, 6):
                p11[pl.ds(row, 16), k * TB : k * TB + TB] = slab[d, 30 + 5 * cb - cb * cb + k]
        return 0

    lax.fori_loop(0, NF, unpack, 0)
    eye = eye_mask()
    for b in range(6):
        cut = slice(b * TB, b * TB + TB)
        for ref, at in ((a, 0), (p11, 2)):
            block = ref[cut, cut]
            row = slab[b // 2, 42][at + b % 2 : at + b % 2 + 1]
            ref[cut, cut] = block + block.T + jnp.where(eye, jnp.broadcast_to(row, (TB, TB)), 0.0)
    factor(a, u, li, n)
    u11[...] = u[:, :PIV]
    for v in range(3):

        @pl.when(pb[v] < 3)
        def _():
            to_col = pl.multiple_of(pb[v] * B, B)
            for half in range(2):
                at = pl.multiple_of(pb[v] * B + half * TB, TB)
                row = slab[v + 3, 42][half : half + 1]
                p11[pl.ds(at, TB), pl.ds(at, TB)] = p11[pl.ds(at, TB), pl.ds(at, TB)] + jnp.where(
                    eye, jnp.broadcast_to(row, (TB, TB)), 0.0
                )
            for w in range(v + 1):
                to_row = pl.multiple_of(pb[w] * B, B)
                gram = dot(
                    u[:, PIV + w * B : PIV + w * B + B], u[:, PIV + v * B : PIV + v * B + B], 0, 0
                )
                p11[pl.ds(to_row, B), pl.ds(to_col, B)] = (
                    p11[pl.ds(to_row, B), pl.ds(to_col, B)] - gram
                )


def first_factor(pb, slab, after):
    n = 2 * PIV
    return pl.pallas_call(
        first_kernel,
        out_shape=[f32s(PIV, PIV), f32s(PIV, PIV), f32s(PIV, TB)],
        in_specs=[SM, VM, ANY],
        out_specs=[VM, VM, VM],
        scratch_shapes=[pltpu.VMEM((PIV, n), f32), pltpu.VMEM((PIV, n), f32)],
        compiler_params=params(),
        name="first",
    )(pb, slab, after)


def second_kernel(own, other, u, li, a):
    a[...] = own[...] + other[...]
    factor(a, u, li, PIV)


def second_factor(own, other):
    return pl.pallas_call(
        second_kernel,
        out_shape=[f32s(PIV, PIV), f32s(PIV, TB)],
        in_specs=[VM, VM],
        out_specs=[VM, VM],
        scratch_shapes=[pltpu.VMEM((PIV, PIV), f32)],
        compiler_params=params(),
        name="second",
    )(own, other)


def solve_kernel(n, u, li, *refs):
    terms, (xt, a) = refs[:n], refs[-2:]
    a[...] = sum((t[...] for t in terms[1:]), terms[0][...])
    for k in range(6):
        o, r = k * TB, k * TB + TB
        x = dot(li[o:r, :], a[o:r, :], 1, 0)
        for j in range(2):
            xt[j * TB : j * TB + TB, o:r] = x[:, j * TB : j * TB + TB].T
        if r < PIV:
            a[r:, :] = a[r:, :] - dot(u[o:r, r:], x, 0, 0)


def solve(u, li, terms, after=()):
    return pl.pallas_call(
        functools.partial(solve_kernel, len(terms)),
        out_shape=f32s(B, PIV),
        in_specs=[VM] * (2 + len(terms)) + [ANY] * len(after),
        out_specs=VM,
        scratch_shapes=[pltpu.VMEM((PIV, B), f32)],
        compiler_params=params(),
        name="solve%d" % len(terms),
    )(u, li, *terms, *after)


def split(x):
    high = x.astype(bf16)
    return high, (x - high.astype(f32)).astype(bf16)


def product(x, y):
    (xh, xl), (yh, yl) = x, y
    one = lambda p, q: lax.dot_general(
        p, q, (((1,), (1,)), ((), ())), preferred_element_type=f32
    )
    return one(xh, yh) + (one(xh, yl) + one(xl, yh))


def write_front(me, xall, u11, low, out):
    sub = lax.broadcasted_iota(jnp.int32, (B, B), 0)
    lane = lax.broadcasted_iota(jnp.int32, (B, B), 1)

    @pl.when(me >= 3)
    def _():
        def clear(k, _):
            out[pl.ds(pl.multiple_of(k * B, B), B), :] = jnp.zeros((B, B), f32)
            return 0

        lax.fori_loop(0, me, clear, 0)

        mine = split(xall[me])

        def update(k, _):
            at = pl.ds(pl.multiple_of((k - 3) * B, B), B)
            value = low(at) - product(split(xall[k]), mine)
            value = jnp.where(jnp.logical_or(k > me, sub >= lane), value, 0.0)
            out[pl.ds(pl.multiple_of(k * B, B), B), :] = value
            return 0

        lax.fori_loop(me, NF, update, 0)

    @pl.when(me < 3)
    def _():
        cols = pl.ds(pl.multiple_of(me * B, B), B)

        def copy(k, _):
            out[pl.ds(pl.multiple_of(k * B, B), B), :] = xall[k, :, cols]
            return 0

        lax.fori_loop(3, NF, copy, 0)
        for ib in range(6):
            for half in range(2):
                jb = 2 * me + half
                src = u11[pl.ds(pl.multiple_of(jb * TB, TB), TB), ib * TB : ib * TB + TB].T
                out[ib * TB : ib * TB + TB, half * TB : half * TB + TB] = jnp.where(
                    ib >= jb, src, 0.0
                )


def extend_kernel(pb, xall, cup, clow, vup, vlow):
    me = lax.axis_index("front")
    vup[...] = cup[...]
    vlow[...] = clow[...]

    def column(v, _):
        @pl.when(jnp.logical_and(pb[v] == me, me >= 3))
        def _():
            mine = split(xall[v + 3])

            def row(w, _):
                q = pb[w]

                @pl.when(q < 3)
                def _():
                    at = pl.ds(pl.multiple_of(q * B, B), B)
                    vup[at, :] = vup[at, :] - dot(xall[w + 3], xall[v + 3], 1, 1)

                @pl.when(q >= me)
                def _():
                    at = pl.ds(pl.multiple_of((q - 3) * B, B), B)
                    vlow[at, :] = vlow[at, :] - product(split(xall[w + 3]), mine)

                return 0

            lax.fori_loop(0, UB, row, 0)

        return 0

    lax.fori_loop(0, UB, column, 0)


def extend_add(pb, xall, cup, clow):
    return pl.pallas_call(
        extend_kernel,
        out_shape=[f32s(PIV, B), f32s(F - PIV, B)],
        in_specs=[SM] + [VM] * 3,
        out_specs=[VM] * 2,
        compiler_params=params(),
        name="extend",
    )(pb, xall, cup, clow)


def leaf_out_kernel(xall, u11, alow, after, out):
    write_front(lax.axis_index("front"), xall, u11, lambda at: alow[at, :], out)


def leaf_output(xall, u11, alow, after):
    return pl.pallas_call(
        leaf_out_kernel,
        out_shape=f32s(F, B),
        in_specs=[VM] * 3 + [ANY],
        out_specs=VM,
        compiler_params=params(),
        cost_estimate=pl.CostEstimate(
            flops=8_000_000_000, bytes_accessed=30_000_000, transcendentals=0
        ),
        name="leafout",
    )(xall, u11, alow, after)


def merged_out_kernel(xown, xother, u11, low0, low1, out, xall):
    me = lax.axis_index("front")
    core = lax.rem(lax.axis_index("leaf"), 2)
    mine = pl.ds(pl.multiple_of(core * TB, TB), TB)
    theirs = pl.ds(pl.multiple_of(TB - core * TB, TB), TB)

    def join(k, _):
        xall[k, mine, :] = xown[k]
        xall[k, theirs, :] = xother[k]
        return 0

    lax.fori_loop(3, NF, join, 0)
    write_front(me, xall, u11, lambda at: low0[at, :] + low1[at, :], out)


def merged_output(xown, xother, u11, low0, low1):
    return pl.pallas_call(
        merged_out_kernel,
        out_shape=f32s(F, B),
        in_specs=[VM] * 5,
        out_specs=VM,
        scratch_shapes=[pltpu.VMEM((NF, B, PIV), f32)],
        compiler_params=params(),
        name="mergedout",
    )(xown, xother, u11, low0, low1)


def gather_kernel(x, out, ss, rs, ls):
    me = lax.axis_index("front")
    y, z = me // 4, lax.rem(me, 4)

    def at(yy, zz):
        return lax.rem(yy + 8, 4) * 4 + lax.rem(zz + 8, 4)

    zr, zl, yr, yl = at(y, z + 1), at(y, z - 1), at(y + 1, z), at(y - 1, z)
    gate = pltpu.get_barrier_semaphore()
    for peer in (zr, zl, yr, yl):
        pl.semaphore_signal(gate, inc=1, device_id={"front": peer}, device_id_type=MESH)
    pl.semaphore_wait(gate, 4)
    half = x.shape[0] // 2
    part = half // 2
    own = pltpu.make_async_copy(x, out.at[me], ls)
    own.start()
    copies = []

    def send(src, dst, peer):
        i = len(copies)
        copy = pltpu.make_async_remote_copy(
            src_ref=src,
            dst_ref=dst,
            send_sem=ss.at[i],
            recv_sem=rs.at[i],
            device_id={"front": peer},
            device_id_type=MESH,
        )
        copy.start()
        copies.append(copy)
        return copy

    a, b = pl.ds(0, half), pl.ds(half, half)
    a0, a1 = pl.ds(0, part), pl.ds(part, part)
    b0, b1 = pl.ds(half, part), pl.ds(half + part, part)

    def pass_on(block, rows, peer):
        return send(out.at[block, rows], out.at[block, rows], peer)

    a1r = send(x.at[a], out.at[me, a], zr)
    a1l = send(x.at[a], out.at[me, a], zl)
    b1r = send(x.at[b], out.at[me, b], yr)
    b1l = send(x.at[b], out.at[me, b], yl)
    a1r.wait_recv()
    a2r = pass_on(zl, a0, zr)
    a1l.wait_recv()
    a2l = pass_on(zr, a1, zl)
    b1r.wait_recv()
    b2r = pass_on(yl, b0, yr)
    b1l.wait_recv()
    b2l = pass_on(yr, b1, yl)
    own.wait()
    zo, yo = at(y, z + 2), at(y + 2, z)
    ar, al, br, bl = [], [], [], []

    def second(block_a, block_b):
        ar.append(pass_on(block_a, a, yr))
        al.append(pass_on(block_a, a, yl))
        br.append(pass_on(block_b, b, zr))
        bl.append(pass_on(block_b, b, zl))

    second(me, me)
    second(zl, yl)
    second(zr, yr)
    for copy in (a2r, a2l, b2r, b2l):
        copy.wait_recv()
    second(zo, yo)
    last = []
    for q, o in enumerate((0, -1, 1, 2)):
        ar[q].wait_recv()
        last.append(pass_on(at(y - 1, z + o), a0, yr))
        al[q].wait_recv()
        last.append(pass_on(at(y + 1, z + o), a1, yl))
        br[q].wait_recv()
        last.append(pass_on(at(y + o, z - 1), b0, zr))
        bl[q].wait_recv()
        last.append(pass_on(at(y + o, z + 1), b1, zl))
    for copy in last:
        copy.wait_recv()
    for copy in copies:
        copy.wait_send()


def gather(x, number):
    return pl.pallas_call(
        gather_kernel,
        out_shape=jax.ShapeDtypeStruct((NF,) + x.shape, x.dtype),
        in_specs=[VM],
        out_specs=VM,
        scratch_shapes=[
            pltpu.SemaphoreType.DMA((40,)),
            pltpu.SemaphoreType.DMA((40,)),
            pltpu.SemaphoreType.DMA,
        ],
        compiler_params=params(collective_id=number, has_side_effects=True),
        name="gather%d" % number,
    )(x)


def exchange(x):
    route = [(i, i ^ 1) for i in range(lax.axis_size("leaf"))]
    return jax.tree.map(lambda v: lax.ppermute(v, "leaf", route), x)


def body(tiles, tile_pos, diag, parent_blocks):
    pos = tile_pos.reshape(-1)
    pb = parent_blocks.reshape(-1)
    diag = diag.reshape(4, TB)
    slab, big0, bigm = pack(pos, pb, tiles.reshape(2, T, TB, TB))
    plan = make_plan(pb, jnp.transpose(tile_pos[:, 0], (0, 2, 1, 3)))
    to_all = lambda x: lax.all_to_all(x, "front", 0, 0, tiled=True)
    slab = slab_sum(plan, to_all(slab), diag)
    big0 = to_all(big0)
    slab = gather(slab.reshape(44 * 16, TB), 1)
    slab, bigm = lax.optimization_barrier((slab, bigm))
    slab = slab.reshape(NF, 44, 16, TB)
    bigm = to_all(bigm)
    aup, alow = leaf_assemble(plan, big0, diag, slab)
    u11, p11, li = first_factor(pb, slab, aup)
    m_u11, m_li = second_factor(p11, exchange(p11))
    xt = solve(u11, li, (aup,), (m_li, bigm))
    xall = lax.all_gather(xt, "front")
    cup, clow = parent_assemble(plan, pb, bigm, slab[:, 42], diag, xt)
    vup, vlow = extend_add(pb, xall, cup, clow)
    sup, slow = exchange((vup, vlow))
    m_xt = solve(m_u11, m_li, (vup, sup))
    core = lax.rem(lax.axis_index("leaf"), 2)
    m_half = gather(lax.dynamic_slice_in_dim(m_xt, core * TB, TB, 0), 2)
    leaf = leaf_output(xall, u11, alow, m_half)
    merged = merged_output(m_half, exchange(m_half), m_u11, vlow, slow)
    return leaf[None], merged[None]


def solution(mesh):
    placed = (
        P(None, "leaf", "front", None, None, None),
        P(None, "leaf", None, None, None),
        P(None, "leaf", "front"),
        P("leaf", None),
    )
    return jax.shard_map(
        body,
        mesh=mesh,
        in_specs=placed,
        out_specs=(P("leaf", None, "front"), P("leaf", None, "front")),
        check_vma=False,
    )
```

```python
import functools

import jax
import jax.numpy as jnp
from jax import lax
from jax.experimental import pallas as pl
from jax.experimental.pallas import tpu as pltpu
from jax.sharding import PartitionSpec as P

F = 4096
B = 256
TB = 128
PIV = 768
UB = 13
T = 24
NF = 16
SCALE = 1.0 / 6144.0
MESH = pl.DeviceIdType.MESH
HI = lax.Precision.HIGHEST
f32 = jnp.float32
bf16 = jnp.bfloat16
VM = pl.BlockSpec(memory_space=pltpu.VMEM)
SM = pl.BlockSpec(memory_space=pltpu.SMEM)
ANY = pl.BlockSpec(memory_space=pl.ANY)
LIMIT = 56 << 20
WIDTH = 8


def params(**more):
    return pltpu.CompilerParams(vmem_limit_bytes=LIMIT, **more)


def f32s(*shape):
    return jax.ShapeDtypeStruct(shape, f32)


def dot(a, b, ca, cb):
    return lax.dot_general(
        a, b, (((ca,), (cb,)), ((), ())), precision=HI, preferred_element_type=f32
    )


def row_col(pos, level, src, t):
    base = (level * NF + src) * 2 * T
    return pos[base + t], pos[base + T + t]


def lifted(pb, index):
    return 2 * pb[jnp.maximum(index - 6, 0) // 2] + lax.rem(index, 2)


def owner(r, c):
    return jnp.where(c >= 6, c, r)


def pack_kernel(pos, pb, tiles, slab, big0, bigm, cnt):
    me = lax.axis_index("front")

    def clear(i, _):
        cnt[i] = 0
        return 0

    lax.fori_loop(0, 64, clear, 0)

    def bump(i):
        old = cnt[i]
        cnt[i] = old + 1
        return old

    def put_slab(value, par, slot):
        for h in range(8):
            slab[par * 8 + h, slot] = value[16 * h : 16 * h + 16]

    def put_big(out, base, counter, r, c, tile, turned):
        dest = owner(r, c) // 2
        slot = bump(counter + dest) + base

        @pl.when(c >= 6)
        def _():
            out[dest, slot] = tile

        @pl.when(c < 6)
        def _():
            out[dest, slot] = turned

    def step(t, _):
        r, c = row_col(pos, 0, me, t)
        tile = tiles[0, t]
        turned = tile.astype(f32).T.astype(bf16)

        @pl.when(jnp.logical_and(c < 6, r < 12))
        def _():
            par = lax.rem(c, 2)
            put_slab(turned, par, bump(48 + par))

        @pl.when(r >= 6)
        def _():
            put_big(big0, 0, 0, r, c, tile, turned)

        @pl.when(c >= 6)
        def _():
            er, ec = lifted(pb, r), lifted(pb, c)

            @pl.when(er < 6)
            def _():
                par = lax.rem(ec, 2)
                put_slab(turned, par, 9 + bump(50 + par))

            @pl.when(er >= 6)
            def _():
                put_big(bigm, 0, 16, er, ec, tile, turned)

        r, c = row_col(pos, 1, me, t)
        tile1 = tiles[1, t]
        turned1 = tile1.astype(f32).T.astype(bf16)

        @pl.when(r < 6)
        def _():
            par = lax.rem(c, 2)
            put_slab(turned1, par, 18 + bump(52 + par))

        @pl.when(r >= 6)
        def _():
            put_big(bigm, 6, 32, r, c, tile1, turned1)

        return 0

    lax.fori_loop(0, T, step, 0)


def pack(pos, pb, tiles):
    return pl.pallas_call(
        pack_kernel,
        out_shape=[
            jax.ShapeDtypeStruct((NF, 27, 16, TB), bf16),
            jax.ShapeDtypeStruct((NF, 6, TB, TB), bf16),
            jax.ShapeDtypeStruct((NF, 12, TB, TB), bf16),
        ],
        in_specs=[SM, SM, VM],
        out_specs=[VM, VM, VM],
        scratch_shapes=[pltpu.SMEM((64,), jnp.int32)],
        compiler_params=params(),
        name="pack",
    )(pos, pb, tiles)


def plan_kernel(pb, pos, out):
    me = lax.axis_index("front")
    half = me // 8
    r0, c0, r1, c1 = pos[0, 0], pos[0, 1], pos[1, 0], pos[1, 1]

    def lift(x):
        block = jnp.maximum(x - 6, 0) // 2
        to = jnp.zeros_like(x)
        for u in range(UB):
            to = jnp.where(block == u, pb[u], to)
        return 2 * to + lax.rem(x, 2)

    er, ec = lift(r0), lift(c0)

    def slab_code(c, r, start, slope):
        cb = c // 2
        return start + r + slope * cb - cb * cb

    def own_code(r, c):
        row = jnp.where(c >= 6, r, c)
        return 4 * row + 2 * lax.rem(owner(r, c), 2) + jnp.where(r == c, 1, 0)

    def own_hit(r, c):
        return (r >= 6) & (owner(r, c) // 2 == me)

    sets = (
        ((c0 < 6) & (r0 < 12) & (lax.rem(c0, 2) == half), slab_code(c0, r0, 0, 11)),
        ((c0 >= 6) & (er < 6) & (lax.rem(ec, 2) == half), slab_code(ec, er, 30, 5)),
        ((r1 < 6) & (lax.rem(c1, 2) == half), slab_code(c1, r1, 30, 5)),
        (own_hit(r0, c0), own_code(r0, c0)),
        ((c0 >= 6) & own_hit(er, ec), own_code(er, ec)),
        (own_hit(r1, c1), own_code(r1, c1)),
    )
    before = lax.broadcasted_iota(jnp.int32, (T, T), 0) < lax.broadcasted_iota(
        jnp.int32, (T, T), 1
    )
    before = before.astype(f32)
    lane = lax.broadcasted_iota(jnp.int32, (NF, TB), 1)
    for i, (hit, code) in enumerate(sets):
        one = jnp.where(hit, 1.0, 0.0)
        rank = dot(one, before, 1, 0)
        code = code.astype(f32)
        table = jnp.where(lane == TB - 1, jnp.sum(one, axis=1, keepdims=True), 0.0)
        for k in range(9):
            pick = jnp.where(rank == k, one * code, 0.0)
            table = jnp.where(lane == k, jnp.sum(pick, axis=1, keepdims=True), table)
        out[NF * i : NF * i + NF, :] = (table + 0.5).astype(jnp.int32)


def make_plan(pb, pos):
    return pl.pallas_call(
        plan_kernel,
        out_shape=jax.ShapeDtypeStruct((6 * NF, TB), jnp.int32),
        in_specs=[SM, VM],
        out_specs=VM,
        compiler_params=params(),
        name="plan",
    )(pb, pos)


def slab_kernel(plan, x, diag, out):
    out[...] = jnp.zeros_like(out)
    for i in range(4):
        out[42, i : i + 1] = diag[i : i + 1]

    def source(s, _):
        for i in range(3):

            def add(k, _, i=i):
                at = plan[i * NF + s, k]
                out[at] = out[at] + SCALE * x[s, 9 * i + k].astype(f32)
                return 0

            lax.fori_loop(0, plan[i * NF + s, TB - 1], add, 0)
        return 0

    lax.fori_loop(0, NF, source, 0)


def slab_sum(plan, x, diag):
    return pl.pallas_call(
        slab_kernel,
        out_shape=f32s(44, 16, TB),
        in_specs=[SM, VM, VM],
        out_specs=VM,
        compiler_params=params(),
        name="slab",
    )(plan, x, diag)


def eye_mask():
    return lax.broadcasted_iota(jnp.int32, (TB, TB), 0) == lax.broadcasted_iota(
        jnp.int32, (TB, TB), 1
    )


def place(up, low, code, value):
    row = code // 4
    col = pl.ds(pl.multiple_of(lax.rem(code // 2, 2) * TB, TB), TB)

    @pl.when(row >= 6)
    def _():
        at = pl.ds(pl.multiple_of((row - 6) * TB, TB), TB)
        low[at, col] = low[at, col] + value

        @pl.when(lax.rem(code, 2) == 1)
        def _():
            low[at, col] = low[at, col] + value.T

    @pl.when(row < 6)
    def _():
        at = pl.ds(pl.multiple_of(row * TB, TB), TB)
        up[at, col] = up[at, col] + value


def add_diag(low, me, row0, row1):
    @pl.when(me >= 3)
    def _():
        for half, row in enumerate((row0, row1)):
            at = pl.multiple_of((me - 3) * B + half * TB, TB)
            cols = slice(half * TB, half * TB + TB)
            low[pl.ds(at, TB), cols] = low[pl.ds(at, TB), cols] + jnp.where(
                eye_mask(), jnp.broadcast_to(row, (TB, TB)), 0.0
            )


def gather_tiles(plan, x, up, low, sets):
    first = sets[0]
    up[...] = jnp.zeros_like(up)
    low[...] = jnp.zeros_like(low)

    def source(s, _):
        for i in sets:

            def add(k, _, i=i):
                place(up, low, plan[i * NF + s, k], SCALE * x[s, 6 * (i - first) + k].astype(f32))
                return 0

            lax.fori_loop(0, plan[i * NF + s, TB - 1], add, 0)
        return 0

    lax.fori_loop(0, NF, source, 0)


def leaf_kernel(plan, x, diag, after, up, low):
    me = lax.axis_index("front")
    gather_tiles(plan, x, up, low, (3,))
    add_diag(low, me, diag[0:1], diag[1:2])


def leaf_assemble(plan, x, diag, after):
    return pl.pallas_call(
        leaf_kernel,
        out_shape=[f32s(PIV, B), f32s(F - PIV, B)],
        in_specs=[SM, VM, VM, ANY],
        out_specs=[VM, VM],
        compiler_params=params(),
        name="leafasm",
    )(plan, x, diag, after)


def parent_kernel(plan, pb, x, extra, diag, after, up, low):
    me = lax.axis_index("front")
    gather_tiles(plan, x, up, low, (4, 5))
    add_diag(low, me, diag[2:3], diag[3:4])

    def extended(u, _):
        @pl.when(pb[u] == me)
        def _():
            rows = extra[u + 3]
            add_diag(low, me, rows[0:1], rows[1:2])

        return 0

    lax.fori_loop(0, UB, extended, 0)


def parent_assemble(plan, pb, x, extra, diag, after):
    return pl.pallas_call(
        parent_kernel,
        out_shape=[f32s(PIV, B), f32s(F - PIV, B)],
        in_specs=[SM, SM, VM, VM, VM, ANY],
        out_specs=[VM, VM],
        compiler_params=params(),
        name="parentasm",
    )(plan, pb, x, extra, diag, after)


def lanes(x, j):
    return jnp.broadcast_to(x[:, j : j + 1], (8, TB))


def rows8(x, i):
    return jnp.broadcast_to(x[i : i + 1, :], (8, TB))


def factor_block(block):
    w = WIDTH
    s_rows = list(block)
    sub = lax.broadcasted_iota(jnp.int32, (8, TB), 0)
    lane = lax.broadcasted_iota(jnp.int32, (8, TB), 1)
    inv_rows = [(lane == sub + 8 * v).astype(f32) for v in range(16)]
    for k0 in range(0, TB, w):
        v0, s = k0 // 8, k0 % 8
        m = {(v, j): lanes(s_rows[v], k0 + j) for v in range(v0, 16) for j in range(w)}
        p = {(i, j): rows8(m[v0, j], s + i) for j in range(w) for i in range(j, w)}
        r_rows = [rows8(s_rows[v0], s + i) for i in range(w)]
        q_rows = [rows8(inv_rows[v0], s + i) for i in range(w)]
        low, scale = {}, []
        for j in range(w):
            d = p[j, j]
            for t in range(j):
                d = d - low[j, t] * low[j, t]
            rs = lax.rsqrt(d)
            scale.append(rs)
            for i in range(j + 1, w):
                x = p[i, j]
                for t in range(j):
                    x = x - low[i, t] * low[j, t]
                low[i, j] = x * rs
        us, ws = [], []
        for i in range(w):
            x, q = r_rows[i], q_rows[i]
            for t in range(i):
                x = x - low[i, t] * us[t]
                q = q - low[i, t] * ws[t]
            us.append(x * scale[i])
            ws.append(q * scale[i])
        for v in range(v0, 16):
            cs = []
            for i in range(w):
                x = m[v, i]
                for t in range(i):
                    x = x - low[i, t] * cs[t]
                cs.append(x * scale[i])
            if v == v0:
                cs = [jnp.where(sub >= s + w, x, 0.0) for x in cs]
            a, b = s_rows[v], inv_rows[v]
            for i in range(w):
                a = a - cs[i] * us[i]
                b = b - cs[i] * ws[i]
            if v == v0:
                for i in range(w):
                    a = jnp.where(sub == s + i, us[i], a)
                    b = jnp.where(sub == s + i, ws[i], b)
            s_rows[v], inv_rows[v] = a, b
    s_rows = [jnp.where(lane >= sub + 8 * v, s_rows[v], 0.0) for v in range(16)]
    return s_rows, inv_rows


def factor(a, u, li, n):
    for k in range(6):
        o = k * TB
        r = o + TB
        us, inv = factor_block([a[o + 8 * v : o + 8 * v + 8, o:r] for v in range(16)])
        for v in range(16):
            u[o + 8 * v : o + 8 * v + 8, o:r] = us[v]
            li[o + 8 * v : o + 8 * v + 8, :] = inv[v]
        if r < n:
            u[o:r, r:n] = dot(li[o:r, :], a[o:r, r:n], 1, 0)
            for q in range(r, PIV, TB):
                a[q : q + TB, q:n] = a[q : q + TB, q:n] - dot(
                    u[o:r, q : q + TB], u[o:r, q:n], 0, 0
                )


def first_kernel(pb, slab, after, u11, p11, li, a, u):
    n = 2 * PIV
    p11[...] = jnp.zeros_like(p11)

    def unpack(d, _):
        for cb in range(3):
            row = pl.multiple_of((2 * cb + d // 8) * TB + 16 * lax.rem(d, 8), 16)
            for k in range(2 * cb, 12):
                a[pl.ds(row, 16), k * TB : k * TB + TB] = slab[d, 11 * cb - cb * cb + k]
            for k in range(2 * cb, 6):
                p11[pl.ds(row, 16), k * TB : k * TB + TB] = slab[d, 30 + 5 * cb - cb * cb + k]
        return 0

    lax.fori_loop(0, NF, unpack, 0)
    eye = eye_mask()
    for b in range(6):
        cut = slice(b * TB, b * TB + TB)
        for ref, at in ((a, 0), (p11, 2)):
            block = ref[cut, cut]
            row = slab[b // 2, 42][at + b % 2 : at + b % 2 + 1]
            ref[cut, cut] = block + block.T + jnp.where(eye, jnp.broadcast_to(row, (TB, TB)), 0.0)
    factor(a, u, li, n)
    u11[...] = u[:, :PIV]
    for v in range(3):

        @pl.when(pb[v] < 3)
        def _():
            to_col = pl.multiple_of(pb[v] * B, B)
            for half in range(2):
                at = pl.multiple_of(pb[v] * B + half * TB, TB)
                row = slab[v + 3, 42][half : half + 1]
                p11[pl.ds(at, TB), pl.ds(at, TB)] = p11[pl.ds(at, TB), pl.ds(at, TB)] + jnp.where(
                    eye, jnp.broadcast_to(row, (TB, TB)), 0.0
                )
            for w in range(v + 1):
                to_row = pl.multiple_of(pb[w] * B, B)
                gram = dot(
                    u[:, PIV + w * B : PIV + w * B + B], u[:, PIV + v * B : PIV + v * B + B], 0, 0
                )
                p11[pl.ds(to_row, B), pl.ds(to_col, B)] = (
                    p11[pl.ds(to_row, B), pl.ds(to_col, B)] - gram
                )


def first_factor(pb, slab, after):
    n = 2 * PIV
    return pl.pallas_call(
        first_kernel,
        out_shape=[f32s(PIV, PIV), f32s(PIV, PIV), f32s(PIV, TB)],
        in_specs=[SM, VM, ANY],
        out_specs=[VM, VM, VM],
        scratch_shapes=[pltpu.VMEM((PIV, n), f32), pltpu.VMEM((PIV, n), f32)],
        compiler_params=params(),
        name="first",
    )(pb, slab, after)


def second_kernel(own, other, u, li, a):
    a[...] = own[...] + other[...]
    factor(a, u, li, PIV)


def second_factor(own, other):
    return pl.pallas_call(
        second_kernel,
        out_shape=[f32s(PIV, PIV), f32s(PIV, TB)],
        in_specs=[VM, VM],
        out_specs=[VM, VM],
        scratch_shapes=[pltpu.VMEM((PIV, PIV), f32)],
        compiler_params=params(),
        name="second",
    )(own, other)


def solve_kernel(n, u, li, *refs):
    terms, (xt, a) = refs[:n], refs[-2:]
    a[...] = sum((t[...] for t in terms[1:]), terms[0][...])
    for k in range(6):
        o, r = k * TB, k * TB + TB
        x = dot(li[o:r, :], a[o:r, :], 1, 0)
        for j in range(2):
            xt[j * TB : j * TB + TB, o:r] = x[:, j * TB : j * TB + TB].T
        if r < PIV:
            a[r:, :] = a[r:, :] - dot(u[o:r, r:], x, 0, 0)


def solve(u, li, terms, after=()):
    return pl.pallas_call(
        functools.partial(solve_kernel, len(terms)),
        out_shape=f32s(B, PIV),
        in_specs=[VM] * (2 + len(terms)) + [ANY] * len(after),
        out_specs=VM,
        scratch_shapes=[pltpu.VMEM((PIV, B), f32)],
        compiler_params=params(),
        name="solve%d" % len(terms),
    )(u, li, *terms, *after)


def split(x):
    high = x.astype(bf16)
    return high, (x - high.astype(f32)).astype(bf16)


def product(x, y):
    (xh, xl), (yh, yl) = x, y
    one = lambda p, q: lax.dot_general(
        p, q, (((1,), (1,)), ((), ())), preferred_element_type=f32
    )
    return one(xh, yh) + (one(xh, yl) + one(xl, yh))


def write_front(me, xall, u11, low, out):
    sub = lax.broadcasted_iota(jnp.int32, (B, B), 0)
    lane = lax.broadcasted_iota(jnp.int32, (B, B), 1)

    @pl.when(me >= 3)
    def _():
        def clear(k, _):
            out[pl.ds(pl.multiple_of(k * B, B), B), :] = jnp.zeros((B, B), f32)
            return 0

        lax.fori_loop(0, me, clear, 0)

        mine = split(xall[me])

        def update(k, _):
            at = pl.ds(pl.multiple_of((k - 3) * B, B), B)
            value = low(at) - product(split(xall[k]), mine)
            value = jnp.where(jnp.logical_or(k > me, sub >= lane), value, 0.0)
            out[pl.ds(pl.multiple_of(k * B, B), B), :] = value
            return 0

        lax.fori_loop(me, NF, update, 0)

    @pl.when(me < 3)
    def _():
        cols = pl.ds(pl.multiple_of(me * B, B), B)

        def copy(k, _):
            out[pl.ds(pl.multiple_of(k * B, B), B), :] = xall[k, :, cols]
            return 0

        lax.fori_loop(3, NF, copy, 0)
        for ib in range(6):
            for half in range(2):
                jb = 2 * me + half
                src = u11[pl.ds(pl.multiple_of(jb * TB, TB), TB), ib * TB : ib * TB + TB].T
                out[ib * TB : ib * TB + TB, half * TB : half * TB + TB] = jnp.where(
                    ib >= jb, src, 0.0
                )


def extend_kernel(pb, xall, cup, clow, vup, vlow):
    me = lax.axis_index("front")
    vup[...] = cup[...]
    vlow[...] = clow[...]

    def column(v, _):
        @pl.when(jnp.logical_and(pb[v] == me, me >= 3))
        def _():
            mine = split(xall[v + 3])

            def row(w, _):
                q = pb[w]

                @pl.when(q < 3)
                def _():
                    at = pl.ds(pl.multiple_of(q * B, B), B)
                    vup[at, :] = vup[at, :] - dot(xall[w + 3], xall[v + 3], 1, 1)

                @pl.when(q >= me)
                def _():
                    at = pl.ds(pl.multiple_of((q - 3) * B, B), B)
                    vlow[at, :] = vlow[at, :] - product(split(xall[w + 3]), mine)

                return 0

            lax.fori_loop(0, UB, row, 0)

        return 0

    lax.fori_loop(0, UB, column, 0)


def extend_add(pb, xall, cup, clow):
    return pl.pallas_call(
        extend_kernel,
        out_shape=[f32s(PIV, B), f32s(F - PIV, B)],
        in_specs=[SM] + [VM] * 3,
        out_specs=[VM] * 2,
        compiler_params=params(),
        name="extend",
    )(pb, xall, cup, clow)


def leaf_out_kernel(xall, u11, alow, after, out):
    write_front(lax.axis_index("front"), xall, u11, lambda at: alow[at, :], out)


def leaf_output(xall, u11, alow, after):
    return pl.pallas_call(
        leaf_out_kernel,
        out_shape=f32s(F, B),
        in_specs=[VM] * 3 + [ANY],
        out_specs=VM,
        compiler_params=params(),
        cost_estimate=pl.CostEstimate(
            flops=8_000_000_000, bytes_accessed=30_000_000, transcendentals=0
        ),
        name="leafout",
    )(xall, u11, alow, after)


def merged_out_kernel(xown, xother, u11, low0, low1, out, xall):
    me = lax.axis_index("front")
    core = lax.rem(lax.axis_index("leaf"), 2)
    mine = pl.ds(pl.multiple_of(core * TB, TB), TB)
    theirs = pl.ds(pl.multiple_of(TB - core * TB, TB), TB)

    def join(k, _):
        xall[k, mine, :] = xown[k]
        xall[k, theirs, :] = xother[k]
        return 0

    lax.fori_loop(3, NF, join, 0)
    write_front(me, xall, u11, lambda at: low0[at, :] + low1[at, :], out)


def merged_output(xown, xother, u11, low0, low1):
    return pl.pallas_call(
        merged_out_kernel,
        out_shape=f32s(F, B),
        in_specs=[VM] * 5,
        out_specs=VM,
        scratch_shapes=[pltpu.VMEM((NF, B, PIV), f32)],
        compiler_params=params(),
        name="mergedout",
    )(xown, xother, u11, low0, low1)


def gather_kernel(x, out, ss, rs, ls):
    me = lax.axis_index("front")
    y, z = me // 4, lax.rem(me, 4)

    def at(yy, zz):
        return lax.rem(yy + 8, 4) * 4 + lax.rem(zz + 8, 4)

    zr, zl, yr, yl = at(y, z + 1), at(y, z - 1), at(y + 1, z), at(y - 1, z)
    gate = pltpu.get_barrier_semaphore()
    for peer in (zr, zl, yr, yl):
        pl.semaphore_signal(gate, inc=1, device_id={"front": peer}, device_id_type=MESH)
    pl.semaphore_wait(gate, 4)
    half = x.shape[0] // 2
    part = half // 2
    own = pltpu.make_async_copy(x, out.at[me], ls)
    own.start()
    copies = []

    def send(src, dst, peer):
        i = len(copies)
        copy = pltpu.make_async_remote_copy(
            src_ref=src,
            dst_ref=dst,
            send_sem=ss.at[i],
            recv_sem=rs.at[i],
            device_id={"front": peer},
            device_id_type=MESH,
        )
        copy.start()
        copies.append(copy)
        return copy

    a, b = pl.ds(0, half), pl.ds(half, half)
    a0, a1 = pl.ds(0, part), pl.ds(part, part)
    b0, b1 = pl.ds(half, part), pl.ds(half + part, part)

    def pass_on(block, rows, peer):
        return send(out.at[block, rows], out.at[block, rows], peer)

    a1r = send(x.at[a], out.at[me, a], zr)
    a1l = send(x.at[a], out.at[me, a], zl)
    b1r = send(x.at[b], out.at[me, b], yr)
    b1l = send(x.at[b], out.at[me, b], yl)
    a1r.wait_recv()
    a2r = pass_on(zl, a0, zr)
    a1l.wait_recv()
    a2l = pass_on(zr, a1, zl)
    b1r.wait_recv()
    b2r = pass_on(yl, b0, yr)
    b1l.wait_recv()
    b2l = pass_on(yr, b1, yl)
    own.wait()
    zo, yo = at(y, z + 2), at(y + 2, z)
    ar, al, br, bl = [], [], [], []

    def second(block_a, block_b):
        ar.append(pass_on(block_a, a, yr))
        al.append(pass_on(block_a, a, yl))
        br.append(pass_on(block_b, b, zr))
        bl.append(pass_on(block_b, b, zl))

    second(me, me)
    second(zl, yl)
    second(zr, yr)
    for copy in (a2r, a2l, b2r, b2l):
        copy.wait_recv()
    second(zo, yo)
    last = []
    for q, o in enumerate((0, -1, 1, 2)):
        ar[q].wait_recv()
        last.append(pass_on(at(y - 1, z + o), a0, yr))
        al[q].wait_recv()
        last.append(pass_on(at(y + 1, z + o), a1, yl))
        br[q].wait_recv()
        last.append(pass_on(at(y + o, z - 1), b0, zr))
        bl[q].wait_recv()
        last.append(pass_on(at(y + o, z + 1), b1, zl))
    for copy in last:
        copy.wait_recv()
    for copy in copies:
        copy.wait_send()


def gather(x, number):
    return pl.pallas_call(
        gather_kernel,
        out_shape=jax.ShapeDtypeStruct((NF,) + x.shape, x.dtype),
        in_specs=[VM],
        out_specs=VM,
        scratch_shapes=[
            pltpu.SemaphoreType.DMA((40,)),
            pltpu.SemaphoreType.DMA((40,)),
            pltpu.SemaphoreType.DMA,
        ],
        compiler_params=params(collective_id=number, has_side_effects=True),
        name="gather%d" % number,
    )(x)


def exchange(x):
    route = [(i, i ^ 1) for i in range(lax.axis_size("leaf"))]
    return jax.tree.map(lambda v: lax.ppermute(v, "leaf", route), x)


def body(tiles, tile_pos, diag, parent_blocks):
    pos = tile_pos.reshape(-1)
    pb = parent_blocks.reshape(-1)
    diag = diag.reshape(4, TB)
    slab, big0, bigm = pack(pos, pb, tiles.reshape(2, T, TB, TB))
    plan = make_plan(pb, jnp.transpose(tile_pos[:, 0], (0, 2, 1, 3)))
    to_all = lambda x: lax.all_to_all(x, "front", 0, 0, tiled=True)
    slab = slab_sum(plan, to_all(slab), diag)
    big0 = to_all(big0)
    slab = gather(slab.reshape(44 * 16, TB), 1)
    slab, bigm = lax.optimization_barrier((slab, bigm))
    slab = slab.reshape(NF, 44, 16, TB)
    bigm = to_all(bigm)
    aup, alow = leaf_assemble(plan, big0, diag, slab)
    u11, p11, li = first_factor(pb, slab, aup)
    m_u11, m_li = second_factor(p11, exchange(p11))
    xt = solve(u11, li, (aup,), (m_li, bigm))
    xall = gather(xt, 3)
    cup, clow = parent_assemble(plan, pb, bigm, slab[:, 42], diag, xt)
    vup, vlow = extend_add(pb, xall, cup, clow)
    sup, slow = exchange((vup, vlow))
    m_xt = solve(m_u11, m_li, (vup, sup))
    core = lax.rem(lax.axis_index("leaf"), 2)
    m_half = gather(lax.dynamic_slice_in_dim(m_xt, core * TB, TB, 0), 2)
    leaf = leaf_output(xall, u11, alow, m_half)
    merged = merged_output(m_half, exchange(m_half), m_u11, vlow, slow)
    return leaf[None], merged[None]


def solution(mesh):
    placed = (
        P(None, "leaf", "front", None, None, None),
        P(None, "leaf", None, None, None),
        P(None, "leaf", "front"),
        P("leaf", None),
    )
    return jax.shard_map(
        body,
        mesh=mesh,
        in_specs=placed,
        out_specs=(P("leaf", None, "front"), P("leaf", None, "front")),
        check_vma=False,
    )
```
